128 devices in a mesh: seq: 8 (over x, core), tp: 16 (over y, z).
Axes of the slice: x: 4, y: 4, z: 4, core: 2. Of those that a mesh axis runs over, the one named last changes fastest.
Arguments:
- inputs: bfloat16 [1024, 16384], P('seq', 'tp'), may hold values from -6 to 6
- gates: bfloat16 [1024, 16384], P('seq', 'tp'), may hold values from -6 to 6
- b_input: bfloat16 [1024, 8, 256], P('seq'), may hold values from -2 to 2
- c_output: bfloat16 [1024, 8, 256], P('seq'), may hold values from -2 to 2
- step_size: float32 [256, 1024], P('tp', 'seq'), as said below
- decay_rate: float32 [256], P('tp'), may hold values from 0 to 0.04, as said below
- skip_gain: float32 [256], P('tp'), may hold values from 0.5 to 1.5
- resets: int32 [1024], P('seq'), may hold values from 0 to 1, as said below
- out_weight: bfloat16 [16384, 8192], P('tp', 'seq'), may hold values from -0.046875 to 0.046875
- final_gain: float32 [8192], replicated, may hold values from 0.5 to 1.5
- unembed: bfloat16 [131072, 8192], P(('seq', 'tp')), may hold values from -12 to 12
- targets: int32 [1024], replicated, may hold values from 0 to 131071
Outputs:
- logprobs: float32 [1024], P(('seq', 'tp'))
The draws below stay inside these ranges and needn't reach their ends.
Inputs may be any that keep to these rules, and one draw needn't show every extreme that they name: `resets`: position 0 starts a response; some response is 512 tokens or longer. `step_size`: Positive. `decay_rate`: Positive.
All inputs are finite; a program needn't handle non-finite values.
Results may differ from the reference program's by a relative error of at most 0.0019.
Values may be sent and summed in bfloat16 or wider, within the bound.
No kernel may reach another device: no remote copies, remote signals or barrier semaphores. Data moves between devices by JAX's collectives and lax.ppermute only.
A program may use at most 128 MiB of HBM per device.

```python
import math
import jax
import jax.numpy as jnp
import numpy as np
from jax import lax

D = 8192
HEADS = 256
HEAD_DIM = 64
STATE = 256
GROUPS = 8
TOK_DEV = 128
SQUEEZED_ITEMS = 1024
VOCAB = 131072


def head_rates(key, fast_odds):
    base_key = jax.random.fold_in(key, 101)
    kind_key, fast_key, slow_key = jax.random.split(base_key, 3)
    is_fast = jax.random.randint(kind_key, (HEADS,), 0, fast_odds) == 0
    fast_rate = jnp.exp(jax.random.uniform(fast_key, (HEADS,), jnp.float32, math.log(1.0 / 50.0), math.log(1.0 / 30.0)))
    slow_rate = jnp.exp(jax.random.uniform(slow_key, (HEADS,), jnp.float32, math.log(0.2 / SQUEEZED_ITEMS), math.log(1.5 / SQUEEZED_ITEMS)))
    return jnp.where(is_fast, fast_rate, slow_rate)


def draw_decay_rate(key, part):
    fast_odds = 2
    return head_rates(key, fast_odds)


def draw_step_size(key, part):
    fading_speeds = head_rates(key, 2)
    key = jax.random.fold_in(key, 2)
    base_key, layout_seed, loss_key = jax.random.split(key, 3)
    starting_shift = jnp.exp(jax.random.uniform(base_key, (HEADS, SQUEEZED_ITEMS), jnp.float32, math.log(0.5), math.log(2.0)))
    spike_index = jax.random.randint(layout_seed, (4,), 0, SQUEEZED_ITEMS)
    element_index = jnp.arange(SQUEEZED_ITEMS, dtype=jnp.int32)
    spike_markers = jnp.any(element_index[:, None] == spike_index[None, :], axis=1)
    objective_amount_total = jax.random.uniform(loss_key, (HEADS, SQUEEZED_ITEMS), jnp.float32, 0.22, 0.69)
    return starting_shift + jnp.where(spike_markers[None, :], objective_amount_total / fading_speeds[:, None], 0.0)


def draw_resets(key, part):
    key = jax.random.fold_in(key, 3)
    flag_key, zone_key = jax.random.split(key, 2)
    flags = (jax.random.randint(flag_key, (SQUEEZED_ITEMS,), 0, TOK_DEV) == 0).astype(jnp.int32)
    zone_start = jax.random.randint(zone_key, (), 0, SQUEEZED_ITEMS - SQUEEZED_ITEMS // 2 + 1)
    element_index = jnp.arange(SQUEEZED_ITEMS, dtype=jnp.int32)
    inside = (element_index > zone_start) & (element_index < zone_start + SQUEEZED_ITEMS // 2)
    quiet = jnp.where(inside, 0, flags)
    return jnp.where(element_index == 0, 1, quiet).astype(jnp.int32)


def draw_unembed(key, part):
    key = jax.random.fold_in(key, 4)
    entry_key = key
    entry_scale = 3.0 / math.sqrt(D)
    entries = jax.random.truncated_normal(entry_key, -4.0, 4.0, (VOCAB, D), jnp.float32)
    row_scale = entry_scale * jnp.ones((VOCAB,), jnp.float32)
    scaled = jnp.clip(entries * row_scale[:, None], -11.5, 11.5)
    return scaled.astype(jnp.bfloat16)


def touch_ends(drawn, own_key, least, top_value):
    place = [jax.random.randint(jax.random.fold_in(own_key, axis), (), 0, length) for axis, length in enumerate(drawn.shape)]
    longest = drawn.shape.index(max(drawn.shape))
    neighbour = place[:longest] + [(place[longest] + 1) % drawn.shape[longest]] + place[longest + 1:]
    return drawn.at[tuple(place)].set(least).at[tuple(neighbour)].set(top_value)


def steps_of(rng, extent, pieces, low, high):
    loudness = 1.0
    for dim, blocks in pieces:
        draws = jax.random.uniform(jax.random.fold_in(jax.random.fold_in(rng, 6), dim), (blocks,), jnp.float32, low / len(pieces), high / len(pieces))
        loudness = loudness * jnp.repeat(jnp.exp(draws), extent[dim] // blocks).reshape((-1,) + (1,) * (len(extent) - 1 - dim))
    return loudness


def ranked_wide(stream_key, extent, number_of, skew):
    weights = [min(1 << octave, number_of + 1 - (1 << octave)) * (1 << 20) // math.isqrt((1 << octave) ** skew) + 1 for octave in range((number_of + 1).bit_length()) if 1 << octave <= number_of]
    width = 1 + sum(weights) // (1 << 30)
    table = np.cumsum(np.array([max(1, weight // width) for weight in weights]))
    lot = jax.random.randint(jax.random.fold_in(stream_key, 1), extent, 0, int(table[len(weights) - 1]))
    start = jnp.left_shift(1, jnp.searchsorted(jnp.asarray(table, jnp.int32), lot, side="right").astype(jnp.int32))
    grade = start - 1 + jax.random.randint(jax.random.fold_in(stream_key, 4), extent, 0, 1 << 30) % jnp.minimum(start, number_of + 1 - start)
    return jax.random.permutation(jax.random.fold_in(stream_key, 2), number_of)[grade].astype(jnp.int32)


def noise(rng, shape, scale, limit, cuts=(), held_as=jnp.bfloat16):
    values = jax.random.normal(rng, shape, jnp.float32) * scale
    if len(cuts) > 0:
        values = steps_of(rng, shape, cuts, -0.22, 0.18) * values
    return jnp.clip(values, min=-limit, max=limit).astype(held_as)


def setup_inputs(seed: int = 0) -> dict:
    streams_of = jax.random.split(jax.random.key(seed), 13)
    return {
        "inputs": noise(streams_of[0], (SQUEEZED_ITEMS, HEADS * HEAD_DIM), 1.0, 6.0, ((0, 8), (1, 16))),
        "gates": noise(streams_of[1], (SQUEEZED_ITEMS, HEADS * HEAD_DIM), 1.0, 6.0, ((0, 8), (1, 16))),
        "b_input": noise(streams_of[2], (SQUEEZED_ITEMS, GROUPS, STATE), 0.3, 2.0, ((0, 8),)),
        "c_output": noise(streams_of[3], (SQUEEZED_ITEMS, GROUPS, STATE), 0.3, 2.0, ((0, 8),)),
        "step_size": draw_step_size(jax.random.fold_in(streams_of[12], 71), 0),
        "decay_rate": draw_decay_rate(jax.random.fold_in(streams_of[12], 71), 0),
        "skip_gain": jnp.clip(0.5 + 1.0 * jax.random.uniform(streams_of[6], (HEADS,), jnp.float32) ** steps_of(streams_of[6], (HEADS,), ((0, 16),), -0.2, 0.2), 0.5, 1.5),
        "resets": draw_resets(jax.random.fold_in(streams_of[12], 71), 0),
        "out_weight": noise(streams_of[8], (HEADS * HEAD_DIM, D), (HEADS * HEAD_DIM) ** -0.5, 0.046875, ((0, 16), (1, 8))),
        "final_gain": jnp.clip(1.0 + 0.1 * jax.random.normal(streams_of[9], (D,), jnp.float32), 0.5, 1.5),
        "unembed": draw_unembed(jax.random.fold_in(streams_of[12], 71), 0),
        "targets": touch_ends(ranked_wide(streams_of[11], (SQUEEZED_ITEMS,), VOCAB, 2), jax.random.fold_in(streams_of[11], 3), 0, VOCAB - 1).astype(jnp.int32),
    }


input_cap = 1.5

def reference(inputs, gates, b_input, c_output, step_size, decay_rate, skip_gain, resets, out_weight, final_gain, unembed, targets):
    per_group = HEADS // GROUPS
    features = inputs.astype(jnp.float32).reshape(SQUEEZED_ITEMS, HEADS, HEAD_DIM)
    b_heads = jnp.repeat(b_input.astype(jnp.float32), per_group, axis=1)
    c_heads = jnp.repeat(c_output.astype(jnp.float32), per_group, axis=1)
    steps_th = step_size.T
    keeping = 1.0 - resets.astype(jnp.float32)
    decay = jnp.exp(-decay_rate[None, :] * steps_th) * keeping[:, None]
    feed = jnp.minimum(steps_th, input_cap)[:, :, None] * features

    def advance(state_now, item_now):
        decay_now, b_now, c_now, feed_now = item_now
        state_now = decay_now[:, None, None] * state_now + b_now[:, :, None] * feed_now[:, None, :]
        result_now = jnp.einsum('hn,hnp->hp', c_now, state_now, precision=lax.Precision.HIGHEST)
        return (state_now, result_now)
    start_state = jnp.zeros((HEADS, STATE, HEAD_DIM), jnp.float32)
    final_state, outputs = lax.scan(advance, start_state, (decay, b_heads, c_heads, feed))
    mixer = outputs + skip_gain[None, :, None] * features
    mixer = mixer.reshape(SQUEEZED_ITEMS, HEADS * HEAD_DIM)
    gated = (mixer * jax.nn.silu(gates.astype(jnp.float32))).astype(jnp.bfloat16)
    projected = jnp.dot(gated, out_weight, preferred_element_type=jnp.float32)
    spread = lax.optimization_barrier(jnp.mean(projected * projected, axis=1, keepdims=True))
    normed = (projected * lax.rsqrt(spread + 1e-05) * final_gain[None, :]).astype(jnp.bfloat16)
    logits = jnp.dot(normed, unembed.T, preferred_element_type=jnp.float32)
    totals = jax.nn.logsumexp(logits, axis=1)
    picked = jnp.take_along_axis(logits, targets[:, None], axis=1)[:, 0]
    return picked - totals
```

```python
import functools

import jax
import jax.numpy as jnp
from jax import lax
from jax.experimental import pallas as pl
from jax.experimental.pallas import tpu as pltpu
from jax.sharding import Mesh
from jax.sharding import PartitionSpec as P

HEADS_DEV = 16
HEAD_DIM = 64
CHANNELS = 1024
STATE = 256
BLOCK = 128
TOKENS = 512
COLS = 2048
QUARTER = 512
TILE = 512
WORDS = 1024
INPUT_CAP = 1.5
FAR = 100.0

AXES = ("x", "core", "y", "z")
f32 = jnp.float32
bf16 = jnp.bfloat16

B0, C0, PACK = 1024, 1280, 1536
PACK_ROWS = 144


def along(axis, hop):
    pairs = []
    for x in range(4):
        for c in range(2):
            for y in range(4):
                for z in range(4):
                    to = {"x": x, "c": c, "y": y, "z": z}
                    name = axis
                    if axis == "a":
                        name = "yz"[c]
                    elif axis == "b":
                        name = "zy"[c]
                    to[name] = (to[name] + hop) % (2 if name == "c" else 4)
                    here = ((x * 2 + c) * 4 + y) * 4 + z
                    there = ((to["x"] * 2 + to["c"]) * 4 + to["y"]) * 4 + to["z"]
                    pairs.append((here, there))
    return pairs


def send(value, axis, hop):
    return lax.ppermute(value, AXES, along(axis, hop))


def in_hbm(value):
    return pltpu.with_memory_space_constraint(value, pltpu.HBM)


def split_dot(a, b):
    high = a.astype(bf16)
    low = (a - high.astype(f32)).astype(bf16)
    return jnp.dot(high, b, preferred_element_type=f32) + jnp.dot(
        low, b, preferred_element_type=f32
    )


def mixer_kernel(
    place_ref,
    rate_ref,
    skip_ref,
    expand_ref,
    p0, p1, p2, p3, s0, s1, s2, s3,
    out_ref,
    pack, until_rows, weight_rows, count_rows, turned, state, entered, sems,
):
    mine, core = place_ref[0], place_ref[1]
    copies = []
    for slot, hop in enumerate((0, 1, 3, 2)):
        chip = lax.rem(mine + 4 - hop, 4)
        own, other = (p0, p1, p2, p3)[slot], (s0, s1, s2, s3)[slot]
        copies.append(pltpu.make_async_copy(own, pack.at[2 * chip + core], sems.at[slot]))
        copies.append(pltpu.make_async_copy(other, pack.at[2 * chip + 1 - core], sems.at[4 + slot]))
    for copy in copies:
        copy.start()
    state[...] = jnp.zeros_like(state)
    rows = lax.broadcasted_iota(jnp.int32, (BLOCK, BLOCK), 0)
    lanes = lax.broadcasted_iota(jnp.int32, (BLOCK, BLOCK), 1)
    causal = rows >= lanes
    upto = (rows <= lanes).astype(bf16)
    after = (rows > lanes).astype(bf16)
    expand = expand_ref[...]
    for copy in copies:
        copy.wait()

    def per_head(k):
        parts = [pack[p, BLOCK:, k * BLOCK : (k + 1) * BLOCK] for p in range(8)]
        return jnp.concatenate(parts, axis=0)

    step = per_head(0).astype(f32) + per_head(1).astype(f32) + per_head(2).astype(f32)
    resets = per_head(3)
    loss = jnp.minimum(rate_ref[...] * step, FAR)
    high = loss.astype(bf16)
    mid = (loss - high.astype(f32)).astype(bf16)
    low = (loss - high.astype(f32) - mid.astype(f32)).astype(bf16)
    dot = functools.partial(jnp.dot, preferred_element_type=f32)
    until = dot(high, upto) + dot(mid, upto) + dot(low, upto)
    later = dot(high, after) + dot(mid, after) + dot(low, after)
    count = dot(resets, upto)
    weight = jnp.minimum(step, INPUT_CAP)
    until_rows[...] = until
    weight_rows[...] = weight
    count_rows[...] = count
    turned[0] = jnp.transpose(until)
    turned[1] = jnp.transpose(count)
    turned[2] = jnp.transpose(jnp.where(count == 0.0, jnp.exp(-until), 0.0))
    turned[3] = jnp.transpose(jnp.where(dot(resets, after) == 0.0, weight * jnp.exp(-later), 0.0))

    def added(p):
        back = lax.rem(BLOCK - p * HEADS_DEV, BLOCK)
        inflow = pltpu.roll(turned[3], back, 1)
        entry = pltpu.roll(turned[2, BLOCK - 8 :, :], back, 1)
        features = pack[p, :BLOCK, :B0].astype(f32)
        grown = (features * split_dot(inflow, expand)).astype(bf16)
        new = lax.dot_general(
            pack[p, :BLOCK, B0:C0], grown, (((0,), (0,)), ((), ())), preferred_element_type=f32
        )
        return new, split_dot(entry, expand)[7:8]

    def two_blocks(chip, _):
        new, whole = added(2 * chip)
        before = state[...]
        middle = before * whole + new
        state[...] = middle
        entered[...] = jnp.where(core == 0, before, middle).astype(bf16)

        p = 2 * chip + core
        back = lax.rem(BLOCK - p * HEADS_DEV, BLOCK)
        entry = pltpu.roll(turned[2], back, 1)
        until_t = pltpu.roll(turned[0], back, 1)
        count_t = pltpu.roll(turned[1], back, 1)
        here = pl.ds(pl.multiple_of(p * HEADS_DEV, HEADS_DEV), HEADS_DEV)
        until_p, weight_p = until_rows[here, :], weight_rows[here, :]
        linked = causal & (count_t[:, 0:1] == count_rows[here, :][0:1, :])
        c_block = pack[p, :BLOCK, C0:]
        scores = lax.dot_general(
            c_block,
            pack[p, :BLOCK, B0:C0],
            (((1,), (1,)), ((), ())),
            preferred_element_type=f32,
        )
        scores = jnp.where(linked, scores, 0.0)
        inter = jnp.dot(c_block, entered[...], preferred_element_type=f32)
        inter = inter * split_dot(entry, expand)
        left = lanes < HEAD_DIM
        for pair in range(HEADS_DEV // 2):
            wide = slice(pair * 128, (pair + 1) * 128)
            both = pack[p, :BLOCK, wide]
            mixes = []
            for head in (2 * pair, 2 * pair + 1):
                gap = until_p[head : head + 1, :] - until_t[:, head : head + 1]
                fade = jnp.exp(jnp.minimum(gap, 0.0))
                mixes.append((fade * (scores * weight_p[head : head + 1, :])).astype(bf16))
            zero = jnp.zeros_like(both)
            stacked = jnp.concatenate(
                [jnp.where(left, both, zero), jnp.where(left, zero, both)], axis=0
            )
            intra = jnp.dot(jnp.concatenate(mixes, axis=1), stacked, preferred_element_type=f32)
            mixed = intra + inter[:, wide] + skip_ref[:, wide] * both.astype(f32)
            out_ref[pl.ds(pl.multiple_of(chip * BLOCK, BLOCK), BLOCK), wide] = mixed

        new, whole = added(2 * chip + 1)
        state[...] = state[...] * whole + new
        return 0

    lax.fori_loop(0, 4, two_blocks, 0)


def package_kernel(inputs_ref, b_ref, c_ref, step_ref, resets_ref, out_ref):
    out_ref[:BLOCK, :B0] = inputs_ref[...]
    out_ref[:BLOCK, B0:C0] = b_ref[...]
    out_ref[:BLOCK, C0:] = c_ref[...]
    step = step_ref[...]
    high = step.astype(bf16)
    mid = (step - high.astype(f32)).astype(bf16)
    low = (step - high.astype(f32) - mid.astype(f32)).astype(bf16)
    flags = jnp.broadcast_to(resets_ref[...].astype(f32), step.shape).astype(bf16)
    rest = jnp.zeros((HEADS_DEV, PACK - 4 * BLOCK), bf16)
    out_ref[BLOCK:, :] = jnp.concatenate([high, mid, low, flags, rest], axis=1)


def packaged(inputs, b_block, c_block, step_size, resets):
    vmem = pl.BlockSpec(memory_space=pltpu.VMEM)
    return pl.pallas_call(
        package_kernel,
        in_specs=[vmem] * 5,
        out_specs=vmem,
        out_shape=jax.ShapeDtypeStruct((PACK_ROWS, PACK), bf16),
        compiler_params=pltpu.CompilerParams(vmem_limit_bytes=4 * 2**20),
        cost_estimate=pl.CostEstimate(flops=0, bytes_accessed=10**6, transcendentals=0),
        name="packaged",
    )(inputs, b_block, c_block, step_size, resets)


def mixer(place, rate, skip, expand, packs, other_packs):
    hbm = pl.BlockSpec(memory_space=pltpu.HBM)
    vmem = pl.BlockSpec(memory_space=pltpu.VMEM)
    return pl.pallas_call(
        mixer_kernel,
        out_shape=jax.ShapeDtypeStruct((TOKENS, CHANNELS), f32),
        in_specs=[pl.BlockSpec(memory_space=pltpu.SMEM), vmem, vmem, vmem] + [hbm] * 8,
        out_specs=vmem,
        scratch_shapes=[
            pltpu.VMEM((8, PACK_ROWS, PACK), bf16),
            pltpu.VMEM((BLOCK, BLOCK), f32),
            pltpu.VMEM((BLOCK, BLOCK), f32),
            pltpu.VMEM((BLOCK, BLOCK), f32),
            pltpu.VMEM((4, BLOCK, BLOCK), f32),
            pltpu.VMEM((STATE, CHANNELS), f32),
            pltpu.VMEM((STATE, CHANNELS), bf16),
            pltpu.SemaphoreType.DMA((8,)),
        ],
        compiler_params=pltpu.CompilerParams(vmem_limit_bytes=32 * 2**20),
        cost_estimate=pl.CostEstimate(
            flops=4 * 10**9, bytes_accessed=6 * 2**20, transcendentals=3 * 10**6
        ),
        name="mixer",
    )(place, rate, skip, expand, *packs, *other_packs)


def fetch_columns(place_ref, hop, own, other, weight, sem):
    core, row = place_ref[1], place_ref[2]
    peer = lax.rem(row + hop, 4)
    first = pl.multiple_of(lax.rem(peer, 2) * QUARTER, QUARTER)
    mine = lax.div(peer, 2) == core

    @pl.when(mine)
    def _():
        pltpu.make_async_copy(own.at[:, pl.ds(first, QUARTER)], weight, sem).start()

    @pl.when(jnp.logical_not(mine))
    def _():
        pltpu.make_async_copy(other.at[:, pl.ds(first, QUARTER)], weight, sem).start()


def store_quarters(part, out_ref):
    for b in range(4):
        out_ref[b] = part[:, b * 128 : (b + 1) * 128].astype(out_ref.dtype)


def gate_kernel(hop, place_ref, mixed_ref, g0, g1, g2, g3, own, other, gated_ref, out_ref,
                gates, weight, sems):
    fetch_columns(place_ref, hop, own, other, weight, sems.at[4])
    copies = []
    for slot, back in enumerate((0, 1, 3, 2)):
        chip = lax.rem(place_ref[0] + 4 - back, 4)
        copies.append(
            pltpu.make_async_copy((g0, g1, g2, g3)[slot], gates.at[chip], sems.at[slot])
        )
    for copy in copies:
        copy.start()
    for copy in copies:
        copy.wait()
    for block in range(4):
        rows = slice(block * BLOCK, (block + 1) * BLOCK)
        gate = gates[block].astype(f32)
        gated_ref[rows, :] = (mixed_ref[rows, :] * (gate / (1.0 + jnp.exp(-gate)))).astype(bf16)
    pltpu.make_async_copy(own.at[:, pl.ds(0, QUARTER)], weight, sems.at[4]).wait()
    store_quarters(jnp.dot(gated_ref[...], weight[...], preferred_element_type=f32), out_ref)


def project_kernel(hop, place_ref, gated_ref, own, other, out_ref, weight, sem):
    fetch_columns(place_ref, hop, own, other, weight, sem.at[0])
    pltpu.make_async_copy(own.at[:, pl.ds(0, QUARTER)], weight, sem.at[0]).wait()
    store_quarters(jnp.dot(gated_ref[...], weight[...], preferred_element_type=f32), out_ref)


def gate_and_project(hop, place, mixed, gates, own, other):
    hbm = pl.BlockSpec(memory_space=pltpu.HBM)
    vmem = pl.BlockSpec(memory_space=pltpu.VMEM)
    return pl.pallas_call(
        functools.partial(gate_kernel, hop),
        out_shape=(
            jax.ShapeDtypeStruct((TOKENS, CHANNELS), bf16),
            jax.ShapeDtypeStruct((4, TOKENS, 128), bf16),
        ),
        in_specs=[pl.BlockSpec(memory_space=pltpu.SMEM), vmem] + [hbm] * 6,
        out_specs=(vmem, vmem),
        scratch_shapes=[
            pltpu.VMEM((4, BLOCK, CHANNELS), bf16),
            pltpu.VMEM((CHANNELS, QUARTER), bf16),
            pltpu.SemaphoreType.DMA((5,)),
        ],
        compiler_params=pltpu.CompilerParams(vmem_limit_bytes=24 * 2**20),
        cost_estimate=pl.CostEstimate(
            flops=5 * 10**8, bytes_accessed=6 * 2**20, transcendentals=5 * 10**5
        ),
        name="gate_and_project",
    )(place, mixed, *gates, own, other)


def project(hop, dtype, place, gated, own, other):
    hbm = pl.BlockSpec(memory_space=pltpu.HBM)
    vmem = pl.BlockSpec(memory_space=pltpu.VMEM)
    return pl.pallas_call(
        functools.partial(project_kernel, hop),
        out_shape=jax.ShapeDtypeStruct((4, TOKENS, 128), dtype),
        in_specs=[pl.BlockSpec(memory_space=pltpu.SMEM), vmem, hbm, hbm],
        out_specs=vmem,
        scratch_shapes=[
            pltpu.VMEM((CHANNELS, QUARTER), bf16),
            pltpu.SemaphoreType.DMA((1,)),
        ],
        compiler_params=pltpu.CompilerParams(vmem_limit_bytes=16 * 2**20),
        cost_estimate=pl.CostEstimate(
            flops=5 * 10**8, bytes_accessed=4 * 2**20, transcendentals=0
        ),
        name="project",
    )(place, gated, own, other)


def logits_kernel(first, last, at_ref, *refs):
    refs = list(refs)
    take = lambda n: [refs.pop(0) for _ in range(n)]
    wanted_ref, half0, half1, own, other = take(5)
    acc_in, square_in = (None, None) if first else take(2)
    out_ref = take(1)[0]
    square_ref = None if last else take(1)[0]
    rows, pieces, tile, biggest, summed, picked, sems, tile_sems = take(8)
    columns = [pl.ds(pl.multiple_of(at_ref[k] * QUARTER, QUARTER), QUARTER) for k in range(4)]

    def tile_copies(t):
        return [
            pltpu.make_async_copy(
                (own, other)[t // 2].at[pl.ds((t % 2) * TILE, TILE), columns[k]],
                tile.at[t % 2, :, pl.ds(k * QUARTER, QUARTER)],
                tile_sems.at[t % 2, k],
            )
            for k in range(4)
        ]

    copies = [
        pltpu.make_async_copy(half, pieces.at[h], sems.at[h])
        for h, half in enumerate((half0, half1))
    ]
    for copy in copies + tile_copies(0):
        copy.start()
    for copy in copies:
        copy.wait()
    for h in range(2):
        for xs in range(2):
            for b in range(4):
                k = (h * 2 + xs) * QUARTER + b * 128
                rows[:, k : k + 128] = pieces[h, at_ref[4 + b] * 2 + xs, :TOKENS, :]
    squares = jnp.zeros((4, 128), f32) if first else square_in[...]
    for h in range(2):
        for slot in range(8):
            tail = pieces[h, slot, TOKENS:, :].astype(f32)
            squares = squares + (tail[0:4] + tail[4:8] + tail[8:12])
    if last:
        fixed = lax.rsqrt(squares / 8192.0 + 1e-05)
        scale = jnp.concatenate([fixed[k : k + 1] for k in range(4)], axis=1)
        biggest[...] = jnp.full_like(biggest, -jnp.inf)
        summed[...] = jnp.zeros_like(summed)
        picked[...] = jnp.zeros_like(picked)
    else:
        square_ref[...] = squares

    for t in range(4):
        for copy in tile_copies(t):
            copy.wait()
        if t < 3:
            for copy in tile_copies(t + 1):
                copy.start()
        at = slice(t * TILE, (t + 1) * TILE)
        logits = lax.dot_general(
            tile[t % 2], rows[...], (((1,), (1,)), ((), ())), preferred_element_type=f32
        )
        if not first:
            logits = logits + acc_in[at, :]
        if not last:
            out_ref[at, :] = logits
            continue
        logits = logits * scale
        ids = lax.broadcasted_iota(jnp.int32, logits.shape, 0)
        hit = ids == wanted_ref[...] - (at_ref[8 + t // 2] + (t % 2) * TILE)
        picked[...] += jnp.sum(jnp.where(hit, logits, 0.0), axis=0, keepdims=True)
        top = jnp.maximum(biggest[...], jnp.max(logits, axis=0, keepdims=True))
        summed[...] = summed[...] * jnp.exp(biggest[...] - top) + jnp.sum(
            jnp.exp(logits - top), axis=0, keepdims=True
        )
        biggest[...] = top

    if last:
        out_ref[0:1] = biggest[...] + jnp.log(summed[...])
        out_ref[1:2] = picked[...]


def add_logits(at, wanted, half0, half1, own, other, carried, last):
    first = carried is None
    vmem = pl.BlockSpec(memory_space=pltpu.VMEM)
    hbm = pl.BlockSpec(memory_space=pltpu.HBM)
    anywhere = pl.BlockSpec(memory_space=pl.ANY)
    operands = [at, wanted, half0, half1, own, other]
    in_specs = [pl.BlockSpec(memory_space=pltpu.SMEM), vmem, anywhere, anywhere, hbm, hbm]
    if not first:
        operands += list(carried)
        in_specs += [vmem, vmem]
    if last:
        out_shape = jax.ShapeDtypeStruct((2, TOKENS), f32)
        out_specs = vmem
    else:
        out_shape = (
            pltpu.VMEM((2 * WORDS, TOKENS), f32),
            jax.ShapeDtypeStruct((4, 128), f32),
        )
        out_specs = (vmem, vmem)
    line = pltpu.VMEM((1, TOKENS), f32)
    return pl.pallas_call(
        functools.partial(logits_kernel, first, last),
        in_specs=in_specs,
        out_specs=out_specs,
        out_shape=out_shape,
        scratch_shapes=[
            pltpu.VMEM((TOKENS, 4 * QUARTER), bf16),
            pltpu.VMEM((2, 8, TOKENS + 16, 128), bf16),
            pltpu.VMEM((2, TILE, 4 * QUARTER), bf16),
            line,
            line,
            line,
            pltpu.SemaphoreType.DMA((2,)),
            pltpu.SemaphoreType.DMA((2, 4)),
        ],
        input_output_aliases={} if first or last else {6: 0},
        compiler_params=pltpu.CompilerParams(vmem_limit_bytes=24 * 2**20),
        cost_estimate=pl.CostEstimate(
            flops=4 * 10**9, bytes_accessed=17 * 10**6, transcendentals=10**6 if last else 0
        ),
        name="add_logits",
    )(*operands)


def shards(
    inputs,
    gates,
    b_input,
    c_output,
    step_size,
    decay_rate,
    skip_gain,
    resets,
    out_weight,
    final_gain,
    unembed,
    targets,
):
    x, core = lax.axis_index("x"), lax.axis_index("core")
    y, z = lax.axis_index("y"), lax.axis_index("z")
    a, b = jnp.where(core == 0, y, z), jnp.where(core == 0, z, y)
    group = (y * 4 + z) // 2

    hops = (1, 3, 2)
    package = packaged(
        inputs,
        lax.dynamic_index_in_dim(b_input, group, 1, False),
        lax.dynamic_index_in_dim(c_output, group, 1, False),
        step_size,
        resets[None, :],
    )
    packs = [package] + [send(package, "x", hop) for hop in hops]
    late_weight, _ = lax.optimization_barrier((out_weight, package))
    weight_other = in_hbm(send(late_weight, "c", 1))
    last_pack, *_ = lax.optimization_barrier((packs[1], packs[2], packs[3], weight_other))
    other_packs = [send(pack, "c", 1) for pack in (package, last_pack, packs[2], packs[3])]
    packs = [in_hbm(pack) for pack in packs]
    other_packs = [in_hbm(pack) for pack in other_packs]
    late_gates, *_ = lax.optimization_barrier((gates, *packs))
    late_words, *_ = lax.optimization_barrier((unembed, *other_packs))
    gate_parts = [gates] + [send(late_gates, "x", hop) for hop in hops]
    unembed_other = send(late_words, "c", 1)

    lane = jnp.arange(CHANNELS, dtype=jnp.int32) // HEAD_DIM
    expand = (jnp.arange(BLOCK, dtype=jnp.int32)[:, None] == lane[None, :]).astype(bf16)
    rate = jnp.broadcast_to(jnp.tile(decay_rate, 8)[:, None], (BLOCK, BLOCK))
    skip = jnp.repeat(skip_gain, HEAD_DIM)[None, :]
    place = jnp.stack([x, core, a]).astype(jnp.int32)
    mixed = mixer(place, rate, skip, expand, packs, other_packs)

    gated, part2 = gate_and_project(2, place, mixed, gate_parts, out_weight, weight_other)
    got = [send(part2, "a", 2)]
    for hop in (1, 3):
        part = project(hop, bf16, place, gated, out_weight, weight_other)
        got.append(send(part, "a", hop))
    total = project(0, f32, place, gated, out_weight, weight_other)
    total = total + sum(part.astype(f32) for part in got)

    def share(hop):
        return lax.dynamic_index_in_dim(total, (b + hop) % 4, 0, False)

    projected = sum(send(share(hop).astype(bf16), "b", hop).astype(f32) for hop in (2, 1, 3))
    projected = projected + share(0)

    gain = lax.dynamic_slice_in_dim(final_gain, x * COLS + a * QUARTER + b * 128, 128)
    square = jnp.sum(projected * projected, axis=1).reshape(4, 128)
    high = square.astype(bf16)
    mid = (square - high.astype(f32)).astype(bf16)
    low = (square - high.astype(f32) - mid.astype(f32)).astype(bf16)
    rows = jnp.concatenate(
        [(projected * gain[None, :]).astype(bf16), high, mid, low, jnp.zeros((4, 128), bf16)],
        axis=0,
    )
    near = jnp.stack([rows] + [send(rows, "x", hop) for hop in hops])
    slots = jnp.array([0, 2, 3, 1], jnp.int32)
    slot_of = slots[(jnp.arange(4, dtype=jnp.int32) - b + 4) % 4]
    first_own = ((x * 2 + core) * 16 + y * 4 + z) * WORDS
    first_other = ((x * 2 + 1 - core) * 16 + y * 4 + z) * WORDS
    chips = (x + jnp.array([0, 3, 1, 2], jnp.int32)) % 4
    wanted = lax.dynamic_index_in_dim(targets.reshape(4, 2, BLOCK), core, 1, False)
    wanted = wanted.reshape(1, TOKENS)

    def where_at(hop_top, hop_low):
        top = chips[:2] * 4 + (a + hop_top) % 4
        low = chips[2:] * 4 + (a + hop_low) % 4
        return jnp.concatenate([top, low, slot_of, jnp.stack([first_own, first_other])]).astype(
            jnp.int32
        )

    near, wanted, *places = lax.optimization_barrier(
        (near, wanted, where_at(0, 0), where_at(3, 1), where_at(1, 3), where_at(2, 2))
    )
    line = [near] + [send(near, "b", hop) for hop in hops]
    own_top = jnp.concatenate([piece[:2] for piece in line], axis=0)
    own_low = jnp.concatenate([piece[2:] for piece in line], axis=0)

    step = functools.partial(
        add_logits,
        own=in_hbm(unembed),
        other=in_hbm(unembed_other),
    )
    before_top = send(own_top, "a", 1)
    behind_low = send(own_low, "a", 3)
    carried = step(places[0], wanted, own_top, own_low, carried=None, last=False)
    late_top, late_low, _ = lax.optimization_barrier((own_top, own_low, carried[1]))
    before_low = send(late_low, "a", 1)
    behind_top = send(late_top, "a", 3)
    carried = step(places[1], wanted, before_top, behind_low, carried=carried, last=False)
    relay_top, relay_low, _ = lax.optimization_barrier((before_top, behind_low, carried[1]))
    far_top = send(relay_top, "a", 1)
    far_low = send(relay_low, "a", 3)
    carried = step(places[2], wanted, behind_top, before_low, carried=carried, last=False)
    both = step(places[3], wanted, far_top, far_low, carried=carried, last=True)

    both = both.reshape(2, 64, 8).transpose(1, 0, 2).reshape(64, 16)
    both = lax.all_to_all(both, ("x", "y", "z"), 0, 0, tiled=True).reshape(64, 2, 8)
    top = jnp.max(both[:, 0], axis=0)
    summed = jnp.sum(jnp.exp(both[:, 0] - top[None]), axis=0)
    return jnp.sum(both[:, 1], axis=0) - (top + jnp.log(summed))


def solution(mesh):
    fine = Mesh(mesh.devices.reshape(4, 2, 4, 4), AXES)
    seq, tp = ("x", "core"), ("y", "z")
    return jax.shard_map(
        shards,
        mesh=fine,
        in_specs=(
            P(seq, tp),
            P(seq, tp),
            P(seq, None, None),
            P(seq, None, None),
            P(tp, seq),
            P(tp),
            P(tp),
            P(seq),
            P(tp, seq),
            P(),
            P(AXES, None),
            P(),
        ),
        out_specs=P(AXES),
        check_vma=False,
    )
```
